32 devices in a mesh: groups: 2 (over x), rows: 4 (over y, core), cols: 4 (over z).
Axes of the slice: x: 2, y: 2, z: 4, core: 2. Of those that a mesh axis runs over, the one named last changes fastest.
Arguments:
- pair: bfloat16 [128, 64, 128], P(('groups', 'rows'), 'cols'), parts along dimension 0, may hold values from -6 to 6
- cotangent: bfloat16 [128, 64, 128], P(('groups', 'rows'), 'cols'), parts along dimension 0, may hold values from -6 to 6
- crop_length: int32 [2], P('groups'), parts along dimension 0, may hold values from 32 to 64
- gain_in: float32 [128], replicated, may hold values from 0.1 to 1.9
- w_in: bfloat16 [128, 512], replicated, may hold values from -0.5 to 0.5
- w_gate: bfloat16 [128, 128], replicated, may hold values from -0.5 to 0.5
- product_norm_gain: float32 [128], replicated, may hold values from 0.1 to 1.9
- w_out: bfloat16 [128, 128], replicated, may hold values from -0.5 to 0.5
Outputs:
- update: bfloat16 [128, 64, 128], P(('groups', 'rows'), 'cols'), parts along dimension 0
- pair_grad: bfloat16 [128, 64, 128], P(('groups', 'rows'), 'cols'), parts along dimension 0
- grad_in: float32 [256, 512], P('groups'), parts along dimension 0
- grad_gate: float32 [256, 128], P('groups'), parts along dimension 0
- grad_out: float32 [256, 128], P('groups'), parts along dimension 0
The draws below stay inside these ranges and needn't reach their ends.
There are 2 independent parts, one for each index of `groups`. The reference program is written for one: setup_inputs(seed, part) draws one part's arguments, and reference() takes and returns one part's arrays. A program takes and returns all parts, laid end to end along the dimension named above; an argument that names none is the same for every part. Nothing has to cross between parts.
Inputs may be any that keep to these rules, and one draw needn't show every extreme that they name: The tokens from crop_length[0] on are padding.
All inputs are finite; a program needn't handle non-finite values.
Results may differ from the reference program's by a relative error of at most 0.02.
Values may be sent and summed in bfloat16 or wider, within the bound.
A program may use at most 128 MiB of HBM per device.

```python
import jax
import jax.numpy as jnp
from jax import lax

CZ = 128
CH = 128
TOKENS = 64
N_ROWS = 4


def block_levels(stream_key, extent, split, least, high):
    level, own = 1.0, jax.random.fold_in(stream_key, 6)
    for axis_at, blocks in split:
        draws = jnp.exp(jax.random.uniform(jax.random.fold_in(own, axis_at), (blocks,), jnp.float32, least / len(split), high / len(split)))
        level = level * jnp.repeat(draws, extent[axis_at] // blocks).reshape([-1 if axis == axis_at else 1 for axis in range(len(extent))])
    return level


def scatter_about(key, extent, spread, bound, split=(), held_as=jnp.bfloat16):
    factor_of = block_levels(key, extent, split, -0.22, 0.18) if split else 1.0
    entries = jax.random.normal(key, extent, jnp.float32) * spread * factor_of
    return jnp.minimum(jnp.maximum(entries, -bound), bound).astype(held_as)


def setup_inputs(seed: int = 0, part: int = 0) -> dict:
    arg_keys = jax.random.split(jax.random.key(seed), 9)
    part_splits = jax.random.split(jax.random.fold_in(arg_keys[8], part), 9)
    return {
        "pair": scatter_about(part_splits[0], (TOKENS, TOKENS, CZ), 1.0, 6.0, ((0, 4), (1, 4))),
        "cotangent": scatter_about(part_splits[1], (TOKENS, TOKENS, CZ), 1.0, 6.0, ((0, 4), (1, 4))),
        "crop_length": jax.random.randint(part_splits[2], (1,), TOKENS // 2, TOKENS + 1).astype(jnp.int32),
        "gain_in": jnp.clip(1.0 + 0.18 * jax.random.normal(arg_keys[3], (CZ,), jnp.float32), 0.1, 1.9),
        "w_in": scatter_about(arg_keys[4], (CZ, 4 * CH), CZ ** -0.5, 0.5),
        "w_gate": scatter_about(arg_keys[5], (CZ, CZ), CZ ** -0.5, 0.5),
        "product_norm_gain": jnp.clip(1.0 + 0.18 * jax.random.normal(arg_keys[6], (CH,), jnp.float32), 0.1, 1.9),
        "w_out": scatter_about(arg_keys[7], (CH, CZ), CH ** -0.5, 0.5),
    }


def apply_layer_norm(values, gain):
    centre = values - lax.optimization_barrier(jnp.mean(values, axis=-1, keepdims=True))
    inverse = lax.rsqrt(lax.optimization_barrier(jnp.mean(centre * centre, axis=-1, keepdims=True)) + 1e-05)
    normed = centre * inverse
    return (normed * gain, normed, inverse)

def layer_norm_backward(upstream, gain, normed, inverse):
    scaled = upstream * gain
    return inverse * (scaled - lax.optimization_barrier(jnp.mean(scaled, axis=-1, keepdims=True)) - normed * lax.optimization_barrier(jnp.mean(scaled * normed, axis=-1, keepdims=True)))

def reference(pair, cotangent, crop_length, gain_in, w_in, w_gate, product_norm_gain, w_out):
    f32 = jnp.float32
    to_brain_float = jnp.bfloat16
    positions = jnp.arange(TOKENS, dtype=jnp.int32)
    valid = (positions < crop_length[0]).astype(f32)
    mask = (valid[:, None] * valid[None, :])[:, :, None]
    zn_full, zhat, zinv = apply_layer_norm(pair.astype(f32), gain_in)
    zn_b = zn_full.astype(to_brain_float)
    proj = jnp.dot(zn_b, w_in, preferred_element_type=f32)
    gate = jnp.dot(zn_b, w_gate, preferred_element_type=f32)
    pa_g = proj[..., 0:CH]
    pa_v = proj[..., CH:2 * CH]
    pb_g = proj[..., 2 * CH:3 * CH]
    pb_v = proj[..., 3 * CH:4 * CH]
    sig_a = jax.nn.sigmoid(pa_g)
    sig_b = jax.nn.sigmoid(pb_g)
    left = (sig_a * pa_v * mask).astype(to_brain_float)
    right = (sig_b * pb_v * mask).astype(to_brain_float)
    triangle_update = jnp.einsum('ikh,jkh->ijh', left.astype(f32), right.astype(f32))
    normed_input_full, centred_input, inverse_deviation = apply_layer_norm(triangle_update, product_norm_gain)
    xn_b = normed_input_full.astype(to_brain_float)
    q_out = jnp.dot(xn_b, w_out, preferred_element_type=f32)
    sig_g = jax.nn.sigmoid(gate)
    update = (sig_g * q_out).astype(to_brain_float)
    upstream = cotangent.astype(f32)
    dq_b = (upstream * sig_g).astype(to_brain_float)
    dg_b = (upstream * q_out * sig_g * (1.0 - sig_g)).astype(to_brain_float)
    grad_out = jnp.einsum('ijc,ijd->cd', xn_b.astype(f32), dq_b.astype(f32))
    normed_input_grad = jnp.dot(dq_b, w_out.T, preferred_element_type=f32)
    input_grad_piece = layer_norm_backward(normed_input_grad, product_norm_gain, centred_input, inverse_deviation).astype(to_brain_float)
    grad_left = jnp.einsum('ijh,jkh->ikh', input_grad_piece.astype(f32), right.astype(f32))
    row_block = TOKENS // N_ROWS
    dx_blocks = input_grad_piece.reshape(N_ROWS, row_block, TOKENS, CH)
    left_blocks = left.reshape(N_ROWS, row_block, TOKENS, CH)

    def add_block(total, pieces):
        dx_piece, left_piece = pieces
        term = jnp.einsum('ijh,ikh->jkh', dx_piece.astype(f32), left_piece.astype(f32))
        rounded = lax.optimization_barrier(term.astype(to_brain_float))
        return (total + rounded.astype(f32), None)
    grad_right, _ = lax.scan(add_block, jnp.zeros((TOKENS, TOKENS, CH), f32), (dx_blocks, left_blocks))
    dproj = jnp.concatenate([grad_left * pa_v * mask * sig_a * (1.0 - sig_a), grad_left * sig_a * mask, grad_right * pb_v * mask * sig_b * (1.0 - sig_b), grad_right * sig_b * mask], axis=-1).astype(to_brain_float)
    grad_in = jnp.einsum('ijc,ijd->cd', zn_b.astype(f32), dproj.astype(f32))
    grad_gate = jnp.einsum('ijc,ijd->cd', zn_b.astype(f32), dg_b.astype(f32))
    dzn = jnp.dot(dproj, w_in.T, preferred_element_type=f32) + jnp.dot(dg_b, w_gate.T, preferred_element_type=f32)
    pair_grad = layer_norm_backward(dzn, gain_in, zhat, zinv).astype(to_brain_float)
    return (update, pair_grad, grad_in, grad_gate, grad_out)
```

```python
import functools

import jax
import jax.numpy as jnp
from jax import lax
from jax.experimental import pallas as pl
from jax.experimental.pallas import tpu as pltpu
from jax.sharding import PartitionSpec as P


def apply_layer_norm(values, gain):
    centre = values - jnp.mean(values, axis=-1, keepdims=True)
    inverse = lax.rsqrt(jnp.mean(centre * centre, axis=-1, keepdims=True) + 1e-05)
    normed = centre * inverse
    return (normed * gain, normed, inverse)


def layer_norm_backward(upstream, gain, normed, inverse):
    scaled = upstream * gain
    return inverse * (
        scaled
        - jnp.mean(scaled, axis=-1, keepdims=True)
        - normed * jnp.mean(scaled * normed, axis=-1, keepdims=True)
    )


def per_device(pair, cotangent, crop_length, gain_in, w_in, w_gate, product_norm_gain, w_out):
    f32 = jnp.float32
    to_brain_float = jnp.bfloat16
    row_count = pair.shape[0]
    col_count = pair.shape[1]
    hidden_width = w_out.shape[0]
    row_ids = lax.axis_index("rows") * row_count + jnp.arange(row_count, dtype=jnp.int32)
    col_ids = lax.axis_index("cols") * col_count + jnp.arange(col_count, dtype=jnp.int32)
    row_valid = (row_ids < crop_length[0]).astype(f32)
    col_valid = (col_ids < crop_length[0]).astype(f32)
    mask = (row_valid[:, None] * col_valid[None, :])[:, :, None]
    zn_full, zhat, zinv = apply_layer_norm(pair.astype(f32), gain_in)
    zn_b = zn_full.astype(to_brain_float)
    proj = jnp.dot(zn_b, w_in, preferred_element_type=f32)
    gate = jnp.dot(zn_b, w_gate, preferred_element_type=f32)
    pa_g = proj[..., 0:hidden_width]
    pa_v = proj[..., hidden_width : 2 * hidden_width]
    pb_g = proj[..., 2 * hidden_width : 3 * hidden_width]
    pb_v = proj[..., 3 * hidden_width : 4 * hidden_width]
    sig_a = jax.nn.sigmoid(pa_g)
    sig_b = jax.nn.sigmoid(pb_g)
    left = (sig_a * pa_v * mask).astype(to_brain_float)
    right = (sig_b * pb_v * mask).astype(to_brain_float)
    right_all = lax.all_gather(right, "rows", axis=0, tiled=True)
    partial_value = jnp.einsum("ikh,jkh->ijh", left, right_all, preferred_element_type=f32)
    triangle_update = lax.psum_scatter(
        partial_value.astype(jnp.bfloat16), "cols", scatter_dimension=1, tiled=True
    ).astype(jnp.float32)
    normed_input_full, centred_input, inverse_deviation = apply_layer_norm(
        triangle_update, product_norm_gain
    )
    xn_b = normed_input_full.astype(to_brain_float)
    q_out = jnp.dot(xn_b, w_out, preferred_element_type=f32)
    sig_g = jax.nn.sigmoid(gate)
    update = (sig_g * q_out).astype(to_brain_float)
    upstream = cotangent.astype(f32)
    dq_b = (upstream * sig_g).astype(to_brain_float)
    dg_b = (upstream * q_out * sig_g * (1.0 - sig_g)).astype(to_brain_float)
    local_out = jnp.einsum("ijc,ijd->cd", xn_b, dq_b, preferred_element_type=f32)
    normed_input_grad = jnp.dot(dq_b, w_out.T, preferred_element_type=f32)
    input_grad_piece = layer_norm_backward(
        normed_input_grad, product_norm_gain, centred_input, inverse_deviation
    ).astype(to_brain_float)
    dx_row = lax.all_gather(input_grad_piece, "cols", axis=1, tiled=True)
    grad_left = jnp.einsum("ijh,jkh->ikh", dx_row, right_all, preferred_element_type=f32)
    right_terms = jnp.einsum("ijh,ikh->jkh", dx_row, left, preferred_element_type=f32)
    grad_right = lax.psum_scatter(
        right_terms.astype(jnp.bfloat16), "rows", scatter_dimension=0, tiled=True
    ).astype(jnp.float32)
    dproj = jnp.concatenate(
        [
            grad_left * pa_v * mask * sig_a * (1.0 - sig_a),
            grad_left * sig_a * mask,
            grad_right * pb_v * mask * sig_b * (1.0 - sig_b),
            grad_right * sig_b * mask,
        ],
        axis=-1,
    ).astype(to_brain_float)
    local_in = jnp.einsum("ijc,ijd->cd", zn_b, dproj, preferred_element_type=f32)
    local_gate = jnp.einsum("ijc,ijd->cd", zn_b, dg_b, preferred_element_type=f32)
    grad_in, grad_gate, grad_out = lax.psum((local_in, local_gate, local_out), ("rows", "cols"))
    dzn = jnp.dot(dproj, w_in.T, preferred_element_type=f32) + jnp.dot(
        dg_b, w_gate.T, preferred_element_type=f32
    )
    pair_grad = layer_norm_backward(dzn, gain_in, zhat, zinv).astype(to_brain_float)
    return (update, pair_grad, grad_in, grad_gate, grad_out)


MESH = pl.DeviceIdType.MESH


def last_mean(values):
    return jnp.mean(values, axis=-1, keepdims=True)


def dot_t(lhs, rhs):
    return lax.dot_general(lhs, rhs, (((1,), (1,)), ((), ())), preferred_element_type=jnp.float32)


def fused_kernel(
    n,
    crop_ref,
    pair_ref,
    cot_ref,
    gain_in_ref,
    w_in_ref,
    w_gate_ref,
    gain_x_ref,
    w_out_ref,
    update_ref,
    pair_grad_ref,
    grad_in_ref,
    grad_gate_ref,
    grad_out_ref,
    b_all,
    x_send,
    x_recv,
    dx_all,
    db_send,
    db_recv,
    w_part,
    w_recv,
    w_all,
    left_f,
    right_f,
    dx_f,
    da_f,
    proj_ref,
    zn_ref,
    b_ss,
    b_rs,
    x_ss,
    x_rs,
    dx_ss,
    dx_rs,
    db_ss,
    db_rs,
    ws_ss,
    ws_rs,
    wg_ss,
    wg_rs,
):
    f32, bf16 = jnp.float32, jnp.bfloat16
    blk, _, width = pair_ref.shape
    size = blk * blk
    total = n * n
    share = 2 * width // total
    row = lax.axis_index("rows")
    col = lax.axis_index("cols")
    me = row * n + col

    def peer(step):
        other = lax.rem(me + step, total)
        return other, {"rows": lax.div(other, n), "cols": lax.rem(other, n)}

    barrier = pltpu.get_barrier_semaphore()
    for step in range(1, total):
        _, target = peer(step)
        pl.semaphore_signal(barrier, inc=1, device_id=target, device_id_type=MESH)

    def b_copy(slot, other):
        return pltpu.make_async_remote_copy(
            b_all.at[slot], b_all.at[slot], b_ss.at[other], b_rs.at[slot],
            device_id={"rows": other}, device_id_type=MESH)

    def x_copy(block, slot):
        return pltpu.make_async_remote_copy(
            x_send.at[block], x_recv.at[slot], x_ss.at[block], x_rs.at[slot],
            device_id={"cols": block}, device_id_type=MESH)

    def dx_copy(slot, other):
        return pltpu.make_async_remote_copy(
            dx_all.at[slot], dx_all.at[slot], dx_ss.at[other], dx_rs.at[slot],
            device_id={"cols": other}, device_id_type=MESH)

    def db_copy(block, slot):
        return pltpu.make_async_remote_copy(
            db_send.at[block], db_recv.at[slot], db_ss.at[block], db_rs.at[slot],
            device_id={"rows": block}, device_id_type=MESH)

    def ws_copy(group, other, target, slot):
        return pltpu.make_async_remote_copy(
            w_part.at[group, other], w_recv.at[group, slot],
            ws_ss.at[group, other], ws_rs.at[group, slot],
            device_id=target, device_id_type=MESH)

    def wg_copy(group, other, target, slot):
        return pltpu.make_async_remote_copy(
            w_all.at[group, slot], w_all.at[group, slot],
            wg_ss.at[group, other], wg_rs.at[group, slot],
            device_id=target, device_id_type=MESH)

    def scatter_weights(group, first, second):
        half = total // 2
        w_part[group, 0:half] = first.astype(bf16).reshape(half, share, width)
        w_part[group, half:total] = second.astype(bf16).reshape(half, share, width)

        @pl.loop(1, total)
        def _(step):
            other, target = peer(step)
            ws_copy(group, other, target, me).start()

    def gather_weights(group):
        w_recv[group, me] = w_part[group, me]

        @pl.loop(1, total)
        def _(step):
            other, target = peer(step)
            ws_copy(group, other, target, other).wait_recv()

        summed = jnp.sum(w_recv[group].astype(f32), axis=0)
        w_all[group, me] = summed.astype(bf16)

        @pl.loop(1, total)
        def _(step):
            other, target = peer(step)
            wg_copy(group, other, target, me).start()

    def finish_weights(group):
        @pl.loop(1, total)
        def _(step):
            other, target = peer(step)
            wg_copy(group, other, target, other).wait_recv()

        whole = w_all[group].reshape(2 * width, width).astype(f32)
        return whole[:width], whole[width:]

    gain_in = gain_in_ref[...]
    pair = pair_ref[...].reshape(size, width).astype(f32)
    centre = pair - last_mean(pair)
    zinv = lax.rsqrt(last_mean(centre * centre) + 1e-05)
    zhat = centre * zinv
    zn_f = zhat * gain_in
    zn = zn_f.astype(bf16)
    zn_ref[...] = zn_f.T.astype(bf16)
    crop = crop_ref[0]
    place = lax.broadcasted_iota(jnp.int32, (size, width), 0)
    row_ids = row * blk + lax.div(place, blk)
    col_ids = col * blk + lax.rem(place, blk)
    mask = jnp.where((row_ids < crop) & (col_ids < crop), 1.0, 0.0).astype(f32)
    proj_ref[...] = jnp.dot(zn, w_in_ref[...], preferred_element_type=f32)

    sig_b = jax.nn.sigmoid(proj_ref[:, 2 * width : 3 * width])
    right = (sig_b * proj_ref[:, 3 * width : 4 * width] * mask).astype(bf16)
    b_all[row] = right.reshape(blk, blk, width)

    pl.semaphore_wait(barrier, total - 1)
    for step in range(1, n):
        b_copy(row, lax.rem(row + step, n)).start()

    sig_a = jax.nn.sigmoid(proj_ref[:, 0:width])
    left = (sig_a * proj_ref[:, width : 2 * width] * mask).astype(bf16).astype(f32)
    left_f[...] = left.reshape(blk, blk, width)
    sig_g = jax.nn.sigmoid(jnp.dot(zn, w_gate_ref[...], preferred_element_type=f32))

    for step in range(n):
        block = lax.rem(row + step, n)
        if step > 0:
            b_copy(block, block).wait_recv()
        right_f[...] = jnp.swapaxes(b_all[block].astype(f32), 0, 1)

        @pl.loop(0, blk)
        def _(i):
            line = left_f[i]
            x_send[block, i] = jnp.sum(line[:, None, :] * right_f[...], axis=0).astype(bf16)

        @pl.when(block != col)
        def _():
            x_copy(block, col).start()

    x = x_send[col].astype(f32)
    for step in range(1, n):
        other = lax.rem(col + step, n)
        x_copy(other, other).wait_recv()
        x = x + x_recv[other].astype(f32)
    x = x.reshape(size, width)

    gain_x = gain_x_ref[...]
    w_out = w_out_ref[...]
    cot = cot_ref[...].reshape(size, width).astype(f32)
    centre = x - last_mean(x)
    xinv = lax.rsqrt(last_mean(centre * centre) + 1e-05)
    xhat = centre * xinv
    xn_f = xhat * gain_x
    dq = (cot * sig_g).astype(bf16)
    scaled = dot_t(dq, w_out) * gain_x
    dx = xinv * (scaled - last_mean(scaled) - xhat * last_mean(scaled * xhat))
    dx_all[col] = dx.astype(bf16).reshape(blk, blk, width)
    for step in range(1, n):
        dx_copy(col, lax.rem(col + step, n)).start()
    q_out = jnp.dot(xn_f.astype(bf16), w_out, preferred_element_type=f32)
    update_ref[...] = (sig_g * q_out).astype(bf16).reshape(blk, blk, width)
    dg = (cot * q_out * sig_g * (1.0 - sig_g)).astype(bf16)
    zn_t = zn_ref[...]
    scatter_weights(
        0,
        jnp.dot(zn_t, dg, preferred_element_type=f32),
        jnp.dot(xn_f.T.astype(bf16), dq, preferred_element_type=f32),
    )

    da_f[...] = jnp.zeros_like(da_f)
    for step in range(n):
        block = lax.rem(col + step, n)
        if step > 0:
            dx_copy(block, block).wait_recv()
        dx_f[...] = dx_all[block].astype(f32)
        right_f[...] = b_all[block].astype(f32)

        def over_i(i, db):
            line = dx_f[i][:, None, :]
            da_f[i] += jnp.sum(line * right_f[...], axis=0)
            return db + line * left_f[i][None]

        db = lax.fori_loop(0, blk, over_i, jnp.zeros((blk, blk, width), f32))
        db_send[block] = db.astype(bf16)

        @pl.when(block != row)
        def _():
            db_copy(block, row).start()

    da = da_f[...].reshape(size, width)
    pa_v = proj_ref[:, width : 2 * width]
    d_ag = (da * pa_v * mask * sig_a * (1.0 - sig_a)).astype(bf16)
    d_av = (da * sig_a * mask).astype(bf16)
    scatter_weights(
        1,
        jnp.dot(zn_t, d_ag, preferred_element_type=f32),
        jnp.dot(zn_t, d_av, preferred_element_type=f32),
    )
    dzn = dot_t(dg, w_gate_ref[...]) + dot_t(d_ag, w_in_ref[:, 0:width])
    dzn = dzn + dot_t(d_av, w_in_ref[:, width : 2 * width])
    gather_weights(0)

    db = db_send[row].astype(f32)
    for step in range(1, n):
        other = lax.rem(row + step, n)
        db_copy(other, other).wait_recv()
        db = db + db_recv[other].astype(f32)
    db = db.reshape(size, width)
    pb_v = proj_ref[:, 3 * width : 4 * width]
    d_bg = (db * pb_v * mask * sig_b * (1.0 - sig_b)).astype(bf16)
    d_bv = (db * sig_b * mask).astype(bf16)
    scatter_weights(
        2,
        jnp.dot(zn_t, d_bg, preferred_element_type=f32),
        jnp.dot(zn_t, d_bv, preferred_element_type=f32),
    )
    gather_weights(1)
    dzn = dzn + dot_t(d_bg, w_in_ref[:, 2 * width : 3 * width])
    dzn = dzn + dot_t(d_bv, w_in_ref[:, 3 * width : 4 * width])
    scaled = dzn * gain_in
    pair_grad = zinv * (scaled - last_mean(scaled) - zhat * last_mean(scaled * zhat))
    pair_grad_ref[...] = pair_grad.astype(bf16).reshape(blk, blk, width)
    gather_weights(2)
    grad_gate_ref[...], grad_out_ref[...] = finish_weights(0)
    grad_in_ref[:, 0:width], grad_in_ref[:, width : 2 * width] = finish_weights(1)
    grad_in_ref[:, 2 * width : 3 * width], grad_in_ref[:, 3 * width : 4 * width] = finish_weights(2)

    for step in range(1, n):
        b_copy(row, lax.rem(row + step, n)).wait_send()
        dx_copy(col, lax.rem(col + step, n)).wait_send()
        x_copy(lax.rem(col + step, n), col).wait_send()
        db_copy(lax.rem(row + step, n), row).wait_send()

    @pl.loop(1, total)
    def _(step):
        other, target = peer(step)
        for group in range(3):
            ws_copy(group, other, target, me).wait_send()
            wg_copy(group, other, target, me).wait_send()


def fused_plan(n, pair, cotangent, crop_length, gain_in, w_in, w_gate, product_norm_gain, w_out):
    blk, _, width = pair.shape
    total = n * n
    share = 2 * width // total
    f32, bf16 = jnp.float32, jnp.bfloat16
    shape = jax.ShapeDtypeStruct
    blocks = (n, blk, blk, width)
    shares = (3, total, share, width)
    dma = pltpu.SemaphoreType.DMA
    vmem = pl.BlockSpec(memory_space=pltpu.VMEM)
    return pl.pallas_call(
        functools.partial(fused_kernel, n),
        out_shape=(
            shape(pair.shape, bf16),
            shape(pair.shape, bf16),
            shape(w_in.shape, f32),
            shape(w_gate.shape, f32),
            shape(w_out.shape, f32),
        ),
        in_specs=[pl.BlockSpec(memory_space=pltpu.SMEM)] + [vmem] * 7,
        out_specs=(vmem,) * 5,
        scratch_shapes=[
            pltpu.VMEM(blocks, bf16),
            pltpu.VMEM(blocks, bf16),
            pltpu.VMEM(blocks, bf16),
            pltpu.VMEM(blocks, bf16),
            pltpu.VMEM(blocks, bf16),
            pltpu.VMEM(blocks, bf16),
            pltpu.VMEM(shares, bf16),
            pltpu.VMEM(shares, bf16),
            pltpu.VMEM(shares, bf16),
            pltpu.VMEM(blocks[1:], f32),
            pltpu.VMEM(blocks[1:], f32),
            pltpu.VMEM(blocks[1:], f32),
            pltpu.VMEM(blocks[1:], f32),
            pltpu.VMEM((blk * blk, 4 * width), f32),
            pltpu.VMEM((width, blk * blk), bf16),
        ]
        + [dma((n,))] * 8
        + [dma((3, total))] * 4,
        compiler_params=pltpu.CompilerParams(
            collective_id=0, has_side_effects=True, vmem_limit_bytes=40 * 1024 * 1024
        ),
    )(
        crop_length,
        pair,
        cotangent,
        gain_in.reshape(1, width),
        w_in,
        w_gate,
        product_norm_gain.reshape(1, width),
        w_out,
    )


def choose_plan(n_rows, n_cols, pair, cotangent, crop_length, gain_in, w_in, w_gate, product_norm_gain, w_out):
    args = (pair, cotangent, crop_length, gain_in, w_in, w_gate, product_norm_gain, w_out)
    square = n_rows == n_cols and pair.shape[0] == pair.shape[1] == 16
    even = w_in.shape == (128, 512) and 256 % (16 * n_rows * n_cols) == 0
    return fused_plan(n_rows, *args) if square and even else per_device(*args)


def solution(mesh):
    in_specs = (
        P(("groups", "rows"), "cols", None),
        P(("groups", "rows"), "cols", None),
        P("groups"),
        P(),
        P(),
        P(),
        P(),
        P(),
    )
    out_specs = (
        P(("groups", "rows"), "cols", None),
        P(("groups", "rows"), "cols", None),
        P("groups", None),
        P("groups", None),
        P("groups", None),
    )
    return jax.shard_map(
        functools.partial(choose_plan, mesh.shape["rows"], mesh.shape["cols"]), mesh=mesh, in_specs=in_specs, out_specs=out_specs, check_vma=False
    )
```

```python
import functools

import jax
import jax.numpy as jnp
from jax import lax
from jax.experimental import pallas as pl
from jax.experimental.pallas import tpu as pltpu
from jax.sharding import PartitionSpec as P


def apply_layer_norm(values, gain):
    centre = values - jnp.mean(values, axis=-1, keepdims=True)
    inverse = lax.rsqrt(jnp.mean(centre * centre, axis=-1, keepdims=True) + 1e-05)
    normed = centre * inverse
    return (normed * gain, normed, inverse)


def layer_norm_backward(upstream, gain, normed, inverse):
    scaled = upstream * gain
    return inverse * (
        scaled
        - jnp.mean(scaled, axis=-1, keepdims=True)
        - normed * jnp.mean(scaled * normed, axis=-1, keepdims=True)
    )


def per_device(pair, cotangent, crop_length, gain_in, w_in, w_gate, product_norm_gain, w_out):
    f32 = jnp.float32
    to_brain_float = jnp.bfloat16
    row_count = pair.shape[0]
    col_count = pair.shape[1]
    hidden_width = w_out.shape[0]
    row_ids = lax.axis_index("rows") * row_count + jnp.arange(row_count, dtype=jnp.int32)
    col_ids = lax.axis_index("cols") * col_count + jnp.arange(col_count, dtype=jnp.int32)
    row_valid = (row_ids < crop_length[0]).astype(f32)
    col_valid = (col_ids < crop_length[0]).astype(f32)
    mask = (row_valid[:, None] * col_valid[None, :])[:, :, None]
    zn_full, zhat, zinv = apply_layer_norm(pair.astype(f32), gain_in)
    zn_b = zn_full.astype(to_brain_float)
    proj = jnp.dot(zn_b, w_in, preferred_element_type=f32)
    gate = jnp.dot(zn_b, w_gate, preferred_element_type=f32)
    pa_g = proj[..., 0:hidden_width]
    pa_v = proj[..., hidden_width : 2 * hidden_width]
    pb_g = proj[..., 2 * hidden_width : 3 * hidden_width]
    pb_v = proj[..., 3 * hidden_width : 4 * hidden_width]
    sig_a = jax.nn.sigmoid(pa_g)
    sig_b = jax.nn.sigmoid(pb_g)
    left = (sig_a * pa_v * mask).astype(to_brain_float)
    right = (sig_b * pb_v * mask).astype(to_brain_float)
    right_all = lax.all_gather(right, "rows", axis=0, tiled=True)
    partial_value = jnp.einsum("ikh,jkh->ijh", left, right_all, preferred_element_type=f32)
    triangle_update = lax.psum_scatter(
        partial_value.astype(jnp.bfloat16), "cols", scatter_dimension=1, tiled=True
    ).astype(jnp.float32)
    normed_input_full, centred_input, inverse_deviation = apply_layer_norm(
        triangle_update, product_norm_gain
    )
    xn_b = normed_input_full.astype(to_brain_float)
    q_out = jnp.dot(xn_b, w_out, preferred_element_type=f32)
    sig_g = jax.nn.sigmoid(gate)
    update = (sig_g * q_out).astype(to_brain_float)
    upstream = cotangent.astype(f32)
    dq_b = (upstream * sig_g).astype(to_brain_float)
    dg_b = (upstream * q_out * sig_g * (1.0 - sig_g)).astype(to_brain_float)
    local_out = jnp.einsum("ijc,ijd->cd", xn_b, dq_b, preferred_element_type=f32)
    normed_input_grad = jnp.dot(dq_b, w_out.T, preferred_element_type=f32)
    input_grad_piece = layer_norm_backward(
        normed_input_grad, product_norm_gain, centred_input, inverse_deviation
    ).astype(to_brain_float)
    dx_row = lax.all_gather(input_grad_piece, "cols", axis=1, tiled=True)
    grad_left = jnp.einsum("ijh,jkh->ikh", dx_row, right_all, preferred_element_type=f32)
    right_terms = jnp.einsum("ijh,ikh->jkh", dx_row, left, preferred_element_type=f32)
    grad_right = lax.psum_scatter(
        right_terms.astype(jnp.bfloat16), "rows", scatter_dimension=0, tiled=True
    ).astype(jnp.float32)
    dproj = jnp.concatenate(
        [
            grad_left * pa_v * mask * sig_a * (1.0 - sig_a),
            grad_left * sig_a * mask,
            grad_right * pb_v * mask * sig_b * (1.0 - sig_b),
            grad_right * sig_b * mask,
        ],
        axis=-1,
    ).astype(to_brain_float)
    local_in = jnp.einsum("ijc,ijd->cd", zn_b, dproj, preferred_element_type=f32)
    local_gate = jnp.einsum("ijc,ijd->cd", zn_b, dg_b, preferred_element_type=f32)
    grad_in, grad_gate, grad_out = lax.psum((local_in, local_gate, local_out), ("rows", "cols"))
    dzn = jnp.dot(dproj, w_in.T, preferred_element_type=f32) + jnp.dot(
        dg_b, w_gate.T, preferred_element_type=f32
    )
    pair_grad = layer_norm_backward(dzn, gain_in, zhat, zinv).astype(to_brain_float)
    return (update, pair_grad, grad_in, grad_gate, grad_out)


VMEM_GRANT = 63 * 1024 * 1024
MESH = pl.DeviceIdType.MESH


def last_mean(values):
    return jnp.mean(values, axis=-1, keepdims=True)


def dot_t(lhs, rhs):
    return lax.dot_general(lhs, rhs, (((1,), (1,)), ((), ())), preferred_element_type=jnp.float32)


def fused_kernel(
    n,
    crop_ref,
    pair_hbm,
    cot_hbm,
    gain_in_hbm,
    w_in_hbm,
    w_gate_hbm,
    gain_x_hbm,
    w_out_hbm,
    update_ref,
    pair_grad_ref,
    grad_in_ref,
    grad_gate_ref,
    grad_out_ref,
    pair_all,
    b_all,
    x_send,
    x_recv,
    dx_all,
    db_send,
    db_recv,
    w0_part,
    w0_recv,
    w1_part,
    w1_recv,
    w_all,
    zn_all,
    slope_g,
    slope_v,
    b_sums,
    cot_ref,
    gain_in_ref,
    w_in_ref,
    w_gate_ref,
    gain_x_ref,
    w_out_ref,
    left_f,
    right_f,
    dx_f,
    da_f,
    proj_ref,
    pair_ss,
    pair_rs,
    x_ss,
    x_rs,
    dx_ss,
    dx_rs,
    db_ss,
    db_rs,
    w_ss,
    w_rs,
    in_sem,
):
    f32, bf16 = jnp.float32, jnp.bfloat16
    blk, _, width = pair_hbm.shape
    size = blk * blk
    total = n * n
    share = 2 * width // total
    row = lax.axis_index("rows")
    col = lax.axis_index("cols")
    me = row * n + col

    def peer(step):
        other = lax.rem(me + step, total)
        return other, {"rows": lax.div(other, n), "cols": lax.rem(other, n)}

    def nearest(place):
        for step in range(0, n, 2):
            base = lax.rem(place + step, n)
            yield base
            yield base + 1 - 2 * lax.rem(base, 2)

    near = list(nearest(row))

    fetches = [
        pltpu.make_async_copy(source, target, in_sem.at[at])
        for at, (source, target) in enumerate([
            (pair_hbm, pair_all.at[row]),
            (gain_in_hbm, gain_in_ref),
            (w_in_hbm, w_in_ref),
            (w_gate_hbm, w_gate_ref),
            (cot_hbm, cot_ref),
            (w_out_hbm, w_out_ref),
            (gain_x_hbm, gain_x_ref),
        ])
    ]
    for fetch in fetches:
        fetch.start()

    barrier = pltpu.get_barrier_semaphore()
    for step in range(1, total):
        _, target = peer(step)
        pl.semaphore_signal(barrier, inc=1, device_id=target, device_id_type=MESH)

    def pair_copy(slot, other):
        return pltpu.make_async_remote_copy(
            pair_all.at[slot], pair_all.at[slot], pair_ss.at[other], pair_rs.at[slot],
            device_id={"rows": other}, device_id_type=MESH)

    def x_copy(block, slot):
        return pltpu.make_async_remote_copy(
            x_send.at[block], x_recv.at[slot], x_ss.at[block], x_rs.at[slot],
            device_id={"cols": block}, device_id_type=MESH)

    def dx_copy(slot, other):
        return pltpu.make_async_remote_copy(
            dx_all.at[slot], dx_all.at[slot], dx_ss.at[other], dx_rs.at[slot],
            device_id={"cols": other}, device_id_type=MESH)

    def db_copy(block, slot):
        return pltpu.make_async_remote_copy(
            db_send.at[block], db_recv.at[slot], db_ss.at[block], db_rs.at[slot],
            device_id={"rows": block}, device_id_type=MESH)

    def w_copy(stage, source, target, device):
        return pltpu.make_async_remote_copy(
            source, target, w_ss.at[stage], w_rs.at[stage],
            device_id=device, device_id_type=MESH)

    def w_stage(stage, buffer):
        piece = buffer.at[pl.ds(0, total - 1)]
        return w_copy(stage, piece, piece, peer(1)[1])

    def scatter_weights(stage, outgoing, arriving):
        for step in range(1, total):
            other, target = peer(step)
            w_copy(stage, outgoing.at[other], arriving.at[me], target).start()
        arriving[me] = outgoing[me]

    crop = crop_ref[0]
    place = lax.broadcasted_iota(jnp.int32, (size, width), 0)
    row_ids = lax.div(place, blk)
    col_ok = col * blk + lax.rem(place, blk) < crop

    def mask_of(block):
        return jnp.where((block * blk + row_ids < crop) & col_ok, 1.0, 0.0).astype(f32)

    def normed(block):
        pair = pair_all[block].reshape(size, width).astype(f32)
        centre = pair - last_mean(pair)
        zinv = lax.rsqrt(last_mean(centre * centre) + 1e-05)
        return centre * zinv, zinv

    def prepare(block):
        zhat, _ = normed(block)
        zn_f = zhat * gain_in_ref[...]
        zn = zn_f.astype(bf16)
        mask = mask_of(block)
        pb = jnp.dot(zn, w_in_ref[:, 2 * width : 4 * width], preferred_element_type=f32)
        gated = jax.nn.sigmoid(pb[:, :width]) * mask
        right = (gated * pb[:, width:]).astype(bf16)
        b_all[block] = right.reshape(blk, blk, width)
        zn_all[block] = zn_f.T.astype(bf16)
        slope_v[block] = gated
        slope_g[block] = gated * pb[:, width:] * (1.0 - jax.nn.sigmoid(pb[:, :width]))
        return zn

    for fetch in fetches[:4]:
        fetch.wait()
    zn = prepare(row)
    pl.semaphore_wait(barrier, total - 1)
    for other in near[1:]:
        pair_copy(row, other).start()

    mask = mask_of(row)
    proj_ref[...] = jnp.dot(zn, w_in_ref[:, 0 : 2 * width], preferred_element_type=f32)
    sig_a = jax.nn.sigmoid(proj_ref[:, 0:width])
    left = (sig_a * proj_ref[:, width : 2 * width] * mask).astype(bf16).astype(f32)
    left_f[...] = left.reshape(blk, blk, width)
    sig_g = jax.nn.sigmoid(jnp.dot(zn, w_gate_ref[...], preferred_element_type=f32))

    for step, block in enumerate(near):
        if step > 0:
            pair_copy(block, block).wait_recv()
            prepare(block)
        right_f[...] = jnp.swapaxes(b_all[block].astype(f32), 0, 1)

        @pl.loop(0, blk)
        def _(i):
            line = left_f[i]
            x_send[block, i] = jnp.sum(line[:, None, :] * right_f[...], axis=0).astype(bf16)

        @pl.when(block != col)
        def _():
            x_copy(block, col).start()

    x = x_send[col].astype(f32)
    for step in range(1, n):
        other = lax.rem(col + step, n)
        x_copy(other, other).wait_recv()
        x = x + x_recv[other].astype(f32)
    x = x.reshape(size, width)

    for fetch in fetches[4:]:
        fetch.wait()
    gain_x = gain_x_ref[...]
    w_out = w_out_ref[...]
    cot = cot_ref[...].reshape(size, width).astype(f32)
    centre = x - last_mean(x)
    xinv = lax.rsqrt(last_mean(centre * centre) + 1e-05)
    xhat = centre * xinv
    xn_f = xhat * gain_x
    dq = (cot * sig_g).astype(bf16)
    scaled = dot_t(dq, w_out) * gain_x
    dx = xinv * (scaled - last_mean(scaled) - xhat * last_mean(scaled * xhat))
    dx_all[col] = dx.astype(bf16).reshape(blk, blk, width)
    for step in range(1, n):
        dx_copy(col, lax.rem(col + step, n)).start()
    q_out = jnp.dot(xn_f.astype(bf16), w_out, preferred_element_type=f32)
    update_ref[...] = (sig_g * q_out).astype(bf16).reshape(blk, blk, width)
    dg = (cot * q_out * sig_g * (1.0 - sig_g)).astype(bf16)
    zn_t = zn_all[row]
    half = total // 2
    w0_part[0:half] = (
        jnp.dot(zn_t, dg, preferred_element_type=f32).astype(bf16).reshape(half, share, width))
    w0_part[half:total] = (
        jnp.dot(xn_f.T.astype(bf16), dq, preferred_element_type=f32)
        .astype(bf16).reshape(half, share, width))
    scatter_weights(0, w0_part, w0_recv)

    da_f[...] = jnp.zeros_like(da_f)
    b_sums[...] = jnp.zeros_like(b_sums)
    for step in range(n):
        block = lax.rem(col + step, n)
        if step > 0:
            dx_copy(block, block).wait_recv()
        dx_f[...] = dx_all[block].astype(f32)
        right_f[...] = b_all[block].astype(f32)

        def over_i(i, db):
            line = dx_f[i][:, None, :]
            da_f[i] += jnp.sum(line * right_f[...], axis=0)
            return db + line * left_f[i][None]

        db = lax.fori_loop(0, blk, over_i, jnp.zeros((blk, blk, width), f32))
        db_send[block] = db.astype(bf16)

        @pl.when(block != row)
        def _():
            db_copy(block, row).start()

        terms = db.reshape(size, width)
        zn_block = zn_all[block]
        b_sums[0] += jnp.dot(
            zn_block, (terms * slope_g[block]).astype(bf16), preferred_element_type=f32)
        b_sums[1] += jnp.dot(
            zn_block, (terms * slope_v[block]).astype(bf16), preferred_element_type=f32)

    da = da_f[...].reshape(size, width)
    pa_v = proj_ref[:, width : 2 * width]
    d_ag = (da * pa_v * mask * sig_a * (1.0 - sig_a)).astype(bf16)
    d_av = (da * sig_a * mask).astype(bf16)
    quarter = total // 4
    sums = (
        jnp.dot(zn_t, d_ag, preferred_element_type=f32),
        jnp.dot(zn_t, d_av, preferred_element_type=f32),
        b_sums[0],
        b_sums[1],
    )
    for at, term in enumerate(sums):
        w1_part[at * quarter : (at + 1) * quarter] = (
            term.astype(bf16).reshape(quarter, 2 * share, width))
    scatter_weights(1, w1_part, w1_recv)
    dzn = dot_t(dg, w_gate_ref[...]) + dot_t(d_ag, w_in_ref[:, 0:width])
    dzn = dzn + dot_t(d_av, w_in_ref[:, width : 2 * width])
    w_stage(0, w0_recv).wait_recv()
    w_all[me, 0:share] = jnp.sum(w0_recv[...].astype(f32), axis=0).astype(bf16)
    w_stage(1, w1_recv).wait_recv()
    w_all[me, share : 3 * share] = jnp.sum(w1_recv[...].astype(f32), axis=0).astype(bf16)
    for step in range(1, total):
        _, target = peer(step)
        w_copy(2, w_all.at[me], w_all.at[me], target).start()

    db = db_send[row].astype(f32)
    for other in near[1:]:
        db_copy(other, other).wait_recv()
        db = db + db_recv[other].astype(f32)
    db = db.reshape(size, width)
    d_bg = (db * slope_g[row]).astype(bf16)
    d_bv = (db * slope_v[row]).astype(bf16)
    dzn = dzn + dot_t(d_bg, w_in_ref[:, 2 * width : 3 * width])
    dzn = dzn + dot_t(d_bv, w_in_ref[:, 3 * width : 4 * width])
    zhat, zinv = normed(row)
    scaled = dzn * gain_in_ref[...]
    pair_grad = zinv * (scaled - last_mean(scaled) - zhat * last_mean(scaled * zhat))
    pair_grad_ref[...] = pair_grad.astype(bf16).reshape(blk, blk, width)

    for step in range(1, n):
        pair_copy(row, lax.rem(row + step, n)).wait_send()
        dx_copy(col, lax.rem(col + step, n)).wait_send()
        x_copy(lax.rem(col + step, n), col).wait_send()
        db_copy(lax.rem(row + step, n), row).wait_send()
    w_stage(0, w0_part).wait_send()
    w_stage(1, w1_part).wait_send()
    w_stage(2, w_all).wait_recv()
    early = w_all[:, 0:share].reshape(2 * width, width).astype(f32)
    grad_gate_ref[...], grad_out_ref[...] = early[:width], early[width:]
    late = w_all[:, share : 3 * share].reshape(4 * width, width).astype(f32)
    for at in range(4):
        grad_in_ref[:, at * width : (at + 1) * width] = late[at * width : (at + 1) * width]
    w_stage(2, w_all).wait_send()


def store_kernel(*refs):
    sources, targets, sems = refs[:5], refs[5:10], refs[10]
    copies = [
        pltpu.make_async_copy(source, target, sems.at[at])
        for at, (source, target) in enumerate(zip(sources, targets))
    ]
    for copy in copies:
        copy.start()
    for copy in copies:
        copy.wait()


def fused_plan(n, pair, cotangent, crop_length, gain_in, w_in, w_gate, product_norm_gain, w_out):
    blk, _, width = pair.shape
    total = n * n
    share = 2 * width // total
    f32, bf16 = jnp.float32, jnp.bfloat16
    shape = jax.ShapeDtypeStruct
    blocks = (n, blk, blk, width)
    grad = lambda rows: pltpu.VMEM((total, rows, width), bf16)
    slope = pltpu.VMEM((n, blk * blk, width), f32)
    dma = pltpu.SemaphoreType.DMA
    vmem = pl.BlockSpec(memory_space=pltpu.VMEM)
    hbm = pl.BlockSpec(memory_space=pltpu.HBM)
    out_shape = (
        shape(pair.shape, bf16),
        shape(pair.shape, bf16),
        shape(w_in.shape, f32),
        shape(w_gate.shape, f32),
        shape(w_out.shape, f32),
    )
    results = pl.pallas_call(
        functools.partial(fused_kernel, n),
        out_shape=out_shape,
        in_specs=[pl.BlockSpec(memory_space=pltpu.SMEM)] + [hbm] * 7,
        out_specs=(vmem,) * 5,
        scratch_shapes=[
            pltpu.VMEM(blocks, bf16),
            pltpu.VMEM(blocks, bf16),
            pltpu.VMEM(blocks, bf16),
            pltpu.VMEM(blocks, bf16),
            pltpu.VMEM(blocks, bf16),
            pltpu.VMEM(blocks, bf16),
            pltpu.VMEM(blocks, bf16),
            grad(share),
            grad(share),
            grad(2 * share),
            grad(2 * share),
            grad(3 * share),
            pltpu.VMEM((n, width, blk * blk), bf16),
            slope,
            slope,
            pltpu.VMEM((2, width, width), f32),
            pltpu.VMEM(pair.shape, bf16),
            pltpu.VMEM((1, width), f32),
            pltpu.VMEM(w_in.shape, bf16),
            pltpu.VMEM(w_gate.shape, bf16),
            pltpu.VMEM((1, width), f32),
            pltpu.VMEM(w_out.shape, bf16),
            pltpu.VMEM(blocks[1:], f32),
            pltpu.VMEM(blocks[1:], f32),
            pltpu.VMEM(blocks[1:], f32),
            pltpu.VMEM(blocks[1:], f32),
            pltpu.VMEM((blk * blk, 2 * width), f32),
        ]
        + [dma((n,))] * 8
        + [dma((3,))] * 2
        + [dma((7,))],
        compiler_params=pltpu.CompilerParams(
            collective_id=0, has_side_effects=True, vmem_limit_bytes=VMEM_GRANT
        ),
    )(
        crop_length,
        pair,
        cotangent,
        gain_in.reshape(1, width),
        w_in,
        w_gate,
        product_norm_gain.reshape(1, width),
        w_out,
    )
    return pl.pallas_call(
        store_kernel,
        out_shape=out_shape,
        in_specs=[vmem] * 5,
        out_specs=(hbm,) * 5,
        scratch_shapes=[dma((5,))],
    )(*results)


def choose_plan(n_rows, n_cols, pair, cotangent, crop_length, gain_in, w_in, w_gate, product_norm_gain, w_out):
    args = (pair, cotangent, crop_length, gain_in, w_in, w_gate, product_norm_gain, w_out)
    square = n_rows == n_cols and pair.shape[0] == pair.shape[1] == 16
    even = w_in.shape == (128, 512) and 256 % (16 * n_rows * n_cols) == 0
    return fused_plan(n_rows, *args) if square and even else per_device(*args)


def solution(mesh):
    in_specs = (
        P(("groups", "rows"), "cols", None),
        P(("groups", "rows"), "cols", None),
        P("groups"),
        P(),
        P(),
        P(),
        P(),
        P(),
    )
    out_specs = (
        P(("groups", "rows"), "cols", None),
        P(("groups", "rows"), "cols", None),
        P("groups", None),
        P("groups", None),
        P("groups", None),
    )
    return jax.shard_map(
        functools.partial(choose_plan, mesh.shape["rows"], mesh.shape["cols"]), mesh=mesh, in_specs=in_specs, out_specs=out_specs, check_vma=False
    )
```

```python
import functools

import jax
import jax.numpy as jnp
from jax import lax
from jax.experimental import pallas as pl
from jax.experimental.pallas import tpu as pltpu
from jax.sharding import PartitionSpec as P


def apply_layer_norm(values, gain):
    centre = values - jnp.mean(values, axis=-1, keepdims=True)
    inverse = lax.rsqrt(jnp.mean(centre * centre, axis=-1, keepdims=True) + 1e-05)
    normed = centre * inverse
    return (normed * gain, normed, inverse)


def layer_norm_backward(upstream, gain, normed, inverse):
    scaled = upstream * gain
    return inverse * (
        scaled
        - jnp.mean(scaled, axis=-1, keepdims=True)
        - normed * jnp.mean(scaled * normed, axis=-1, keepdims=True)
    )


def per_device(pair, cotangent, crop_length, gain_in, w_in, w_gate, product_norm_gain, w_out):
    f32 = jnp.float32
    to_brain_float = jnp.bfloat16
    row_count = pair.shape[0]
    col_count = pair.shape[1]
    hidden_width = w_out.shape[0]
    row_ids = lax.axis_index("rows") * row_count + jnp.arange(row_count, dtype=jnp.int32)
    col_ids = lax.axis_index("cols") * col_count + jnp.arange(col_count, dtype=jnp.int32)
    row_valid = (row_ids < crop_length[0]).astype(f32)
    col_valid = (col_ids < crop_length[0]).astype(f32)
    mask = (row_valid[:, None] * col_valid[None, :])[:, :, None]
    zn_full, zhat, zinv = apply_layer_norm(pair.astype(f32), gain_in)
    zn_b = zn_full.astype(to_brain_float)
    proj = jnp.dot(zn_b, w_in, preferred_element_type=f32)
    gate = jnp.dot(zn_b, w_gate, preferred_element_type=f32)
    pa_g = proj[..., 0:hidden_width]
    pa_v = proj[..., hidden_width : 2 * hidden_width]
    pb_g = proj[..., 2 * hidden_width : 3 * hidden_width]
    pb_v = proj[..., 3 * hidden_width : 4 * hidden_width]
    sig_a = jax.nn.sigmoid(pa_g)
    sig_b = jax.nn.sigmoid(pb_g)
    left = (sig_a * pa_v * mask).astype(to_brain_float)
    right = (sig_b * pb_v * mask).astype(to_brain_float)
    right_all = lax.all_gather(right, "rows", axis=0, tiled=True)
    partial_value = jnp.einsum("ikh,jkh->ijh", left, right_all, preferred_element_type=f32)
    triangle_update = lax.psum_scatter(
        partial_value.astype(jnp.bfloat16), "cols", scatter_dimension=1, tiled=True
    ).astype(jnp.float32)
    normed_input_full, centred_input, inverse_deviation = apply_layer_norm(
        triangle_update, product_norm_gain
    )
    xn_b = normed_input_full.astype(to_brain_float)
    q_out = jnp.dot(xn_b, w_out, preferred_element_type=f32)
    sig_g = jax.nn.sigmoid(gate)
    update = (sig_g * q_out).astype(to_brain_float)
    upstream = cotangent.astype(f32)
    dq_b = (upstream * sig_g).astype(to_brain_float)
    dg_b = (upstream * q_out * sig_g * (1.0 - sig_g)).astype(to_brain_float)
    local_out = jnp.einsum("ijc,ijd->cd", xn_b, dq_b, preferred_element_type=f32)
    normed_input_grad = jnp.dot(dq_b, w_out.T, preferred_element_type=f32)
    input_grad_piece = layer_norm_backward(
        normed_input_grad, product_norm_gain, centred_input, inverse_deviation
    ).astype(to_brain_float)
    dx_row = lax.all_gather(input_grad_piece, "cols", axis=1, tiled=True)
    grad_left = jnp.einsum("ijh,jkh->ikh", dx_row, right_all, preferred_element_type=f32)
    right_terms = jnp.einsum("ijh,ikh->jkh", dx_row, left, preferred_element_type=f32)
    grad_right = lax.psum_scatter(
        right_terms.astype(jnp.bfloat16), "rows", scatter_dimension=0, tiled=True
    ).astype(jnp.float32)
    dproj = jnp.concatenate(
        [
            grad_left * pa_v * mask * sig_a * (1.0 - sig_a),
            grad_left * sig_a * mask,
            grad_right * pb_v * mask * sig_b * (1.0 - sig_b),
            grad_right * sig_b * mask,
        ],
        axis=-1,
    ).astype(to_brain_float)
    local_in = jnp.einsum("ijc,ijd->cd", zn_b, dproj, preferred_element_type=f32)
    local_gate = jnp.einsum("ijc,ijd->cd", zn_b, dg_b, preferred_element_type=f32)
    grad_in, grad_gate, grad_out = lax.psum((local_in, local_gate, local_out), ("rows", "cols"))
    dzn = jnp.dot(dproj, w_in.T, preferred_element_type=f32) + jnp.dot(
        dg_b, w_gate.T, preferred_element_type=f32
    )
    pair_grad = layer_norm_backward(dzn, gain_in, zhat, zinv).astype(to_brain_float)
    return (update, pair_grad, grad_in, grad_gate, grad_out)


VMEM_GRANT = 63 * 1024 * 1024
MESH = pl.DeviceIdType.MESH


def last_mean(values):
    return jnp.mean(values, axis=-1, keepdims=True)


def dot_t(lhs, rhs):
    return lax.dot_general(lhs, rhs, (((1,), (1,)), ((), ())), preferred_element_type=jnp.float32)


def fused_kernel(
    n,
    crop_ref,
    pair_hbm,
    cot_hbm,
    gain_in_hbm,
    w_in_hbm,
    w_gate_hbm,
    gain_x_hbm,
    w_out_hbm,
    update_ref,
    pair_grad_ref,
    grad_in_ref,
    grad_gate_ref,
    grad_out_ref,
    pair_all,
    b_all,
    x_send,
    x_recv,
    dx_all,
    db_send,
    db_recv,
    w_part,
    w_recv,
    w_all,
    zn_all,
    slope_g,
    slope_v,
    b_sums,
    cot_ref,
    gain_in_ref,
    w_in_ref,
    w_gate_ref,
    gain_x_ref,
    w_out_ref,
    left_f,
    right_f,
    dx_f,
    da_f,
    proj_ref,
    pair_ss,
    pair_rs,
    x_ss,
    x_rs,
    dx_ss,
    dx_rs,
    db_ss,
    db_rs,
    w_ss,
    w_rs,
    in_sem,
):
    f32, bf16 = jnp.float32, jnp.bfloat16
    blk, _, width = pair_hbm.shape
    size = blk * blk
    total = n * n
    share = 2 * width // total
    row = lax.axis_index("rows")
    col = lax.axis_index("cols")
    me = row * n + col

    def peer(steps):
        to_row, to_col = lax.rem(row + steps[0], n), lax.rem(col + steps[1], n)
        return to_row * n + to_col, {"rows": to_row, "cols": to_col}

    far_first = sorted(range(1, n), key=lambda step: -min(step, n - step))
    peers = [(r, c) for c in far_first + [0] for r in range(n) if r + c > 0]

    def nearest(place):
        for step in range(0, n, 2):
            base = lax.rem(place + step, n)
            yield base
            yield base + 1 - 2 * lax.rem(base, 2)

    near = list(nearest(row))

    fetches = [
        pltpu.make_async_copy(source, target, in_sem.at[at])
        for at, (source, target) in enumerate([
            (pair_hbm, pair_all.at[row]),
            (gain_in_hbm, gain_in_ref),
            (w_in_hbm, w_in_ref),
            (w_gate_hbm, w_gate_ref),
            (cot_hbm, cot_ref),
            (w_out_hbm, w_out_ref),
            (gain_x_hbm, gain_x_ref),
        ])
    ]
    for fetch in fetches:
        fetch.start()

    barrier = pltpu.get_barrier_semaphore()
    for step in peers:
        _, target = peer(step)
        pl.semaphore_signal(barrier, inc=1, device_id=target, device_id_type=MESH)

    def pair_copy(slot, other):
        return pltpu.make_async_remote_copy(
            pair_all.at[slot], pair_all.at[slot], pair_ss.at[other], pair_rs.at[slot],
            device_id={"rows": other}, device_id_type=MESH)

    def x_copy(block, slot):
        return pltpu.make_async_remote_copy(
            x_send.at[block], x_recv.at[slot], x_ss.at[block], x_rs.at[slot],
            device_id={"cols": block}, device_id_type=MESH)

    def dx_copy(slot, other):
        return pltpu.make_async_remote_copy(
            dx_all.at[slot], dx_all.at[slot], dx_ss.at[other], dx_rs.at[slot],
            device_id={"cols": other}, device_id_type=MESH)

    def db_copy(block, slot):
        return pltpu.make_async_remote_copy(
            db_send.at[block], db_recv.at[slot], db_ss.at[block], db_rs.at[slot],
            device_id={"rows": block}, device_id_type=MESH)

    def w_copy(stage, source, target, device):
        return pltpu.make_async_remote_copy(
            source, target, w_ss.at[stage], w_rs.at[stage],
            device_id=device, device_id_type=MESH)

    def w_stage(stage, buffer):
        piece = buffer.at[pl.ds(0, total - 1)]
        return w_copy(stage, piece, piece, peer(peers[0])[1])

    def scatter_weights(stage, outgoing, arriving):
        for step in peers:
            other, target = peer(step)
            w_copy(stage, outgoing.at[other], arriving.at[me], target).start()
        arriving[me] = outgoing[me]

    crop = crop_ref[0]
    place = lax.broadcasted_iota(jnp.int32, (size, width), 0)
    row_ids = lax.div(place, blk)
    col_ok = col * blk + lax.rem(place, blk) < crop

    def mask_of(block):
        return jnp.where((block * blk + row_ids < crop) & col_ok, 1.0, 0.0).astype(f32)

    def normed(block):
        pair = pair_all[block].reshape(size, width).astype(f32)
        centre = pair - last_mean(pair)
        zinv = lax.rsqrt(last_mean(centre * centre) + 1e-05)
        return centre * zinv, zinv

    def prepare(block):
        zhat, _ = normed(block)
        zn_f = zhat * gain_in_ref[...]
        zn = zn_f.astype(bf16)
        mask = mask_of(block)
        pb = jnp.dot(zn, w_in_ref[:, 2 * width : 4 * width], preferred_element_type=f32)
        gated = jax.nn.sigmoid(pb[:, :width]) * mask
        right = (gated * pb[:, width:]).astype(bf16)
        b_all[block] = right.reshape(blk, blk, width)
        zn_all[block] = zn_f.T.astype(bf16)
        slope_v[block] = gated
        slope_g[block] = gated * pb[:, width:] * (1.0 - jax.nn.sigmoid(pb[:, :width]))
        return zn

    for fetch in fetches[:4]:
        fetch.wait()
    zn = prepare(row)
    pl.semaphore_wait(barrier, total - 1)
    for other in near[1:]:
        pair_copy(row, other).start()

    mask = mask_of(row)
    proj_ref[...] = jnp.dot(zn, w_in_ref[:, 0 : 2 * width], preferred_element_type=f32)
    sig_a = jax.nn.sigmoid(proj_ref[:, 0:width])
    left = (sig_a * proj_ref[:, width : 2 * width] * mask).astype(bf16).astype(f32)
    left_f[...] = left.reshape(blk, blk, width)
    sig_g = jax.nn.sigmoid(jnp.dot(zn, w_gate_ref[...], preferred_element_type=f32))

    for step, block in enumerate(near):
        if step > 0:
            pair_copy(block, block).wait_recv()
            prepare(block)
        right_f[...] = jnp.swapaxes(b_all[block].astype(f32), 0, 1)

        @pl.loop(0, blk, unroll=4)
        def _(i):
            line = left_f[i]
            x_send[block, i] = jnp.sum(line[:, None, :] * right_f[...], axis=0).astype(bf16)

        @pl.when(block != col)
        def _():
            x_copy(block, col).start()

    x = x_send[col].astype(f32)
    for step in range(1, n):
        other = lax.rem(col + step, n)
        x_copy(other, other).wait_recv()
        x = x + x_recv[other].astype(f32)
    x = x.reshape(size, width)

    for fetch in fetches[4:]:
        fetch.wait()
    gain_x = gain_x_ref[...]
    w_out = w_out_ref[...]
    cot = cot_ref[...].reshape(size, width).astype(f32)
    centre = x - last_mean(x)
    xinv = lax.rsqrt(last_mean(centre * centre) + 1e-05)
    xhat = centre * xinv
    xn_f = xhat * gain_x
    dq = (cot * sig_g).astype(bf16)
    scaled = dot_t(dq, w_out) * gain_x
    dx = xinv * (scaled - last_mean(scaled) - xhat * last_mean(scaled * xhat))
    dx_all[col] = dx.astype(bf16).reshape(blk, blk, width)
    for step in far_first:
        dx_copy(col, lax.rem(col + step, n)).start()
    q_out = jnp.dot(xn_f.astype(bf16), w_out, preferred_element_type=f32)
    update_ref[...] = (sig_g * q_out).astype(bf16).reshape(blk, blk, width)
    dg = (cot * q_out * sig_g * (1.0 - sig_g)).astype(bf16)
    zn_t = zn_all[row]
    half = total // 2
    w_part[0:half, 0:share] = (
        jnp.dot(zn_t, dg, preferred_element_type=f32).astype(bf16).reshape(half, share, width))
    w_part[half:total, 0:share] = (
        jnp.dot(xn_f.T.astype(bf16), dq, preferred_element_type=f32)
        .astype(bf16).reshape(half, share, width))

    da_f[...] = jnp.zeros_like(da_f)
    b_sums[...] = jnp.zeros_like(b_sums)
    for step in [0] + far_first[::-1]:
        block = lax.rem(col + step, n)
        if step > 0:
            dx_copy(block, block).wait_recv()
        dx_f[...] = dx_all[block].astype(f32)
        right_f[...] = b_all[block].astype(f32)

        def over_i(i, db):
            line = dx_f[i][:, None, :]
            da_f[i] += jnp.sum(line * right_f[...], axis=0)
            return db + line * left_f[i][None]

        db = lax.fori_loop(0, blk, over_i, jnp.zeros((blk, blk, width), f32), unroll=2)
        db_send[block] = db.astype(bf16)

        @pl.when(block != row)
        def _():
            db_copy(block, row).start()

        terms = db.reshape(size, width)
        zn_block = zn_all[block]
        b_sums[0] += jnp.dot(
            zn_block, (terms * slope_g[block]).astype(bf16), preferred_element_type=f32)
        b_sums[1] += jnp.dot(
            zn_block, (terms * slope_v[block]).astype(bf16), preferred_element_type=f32)

    da = da_f[...].reshape(size, width)
    pa_v = proj_ref[:, width : 2 * width]
    d_ag = (da * pa_v * mask * sig_a * (1.0 - sig_a)).astype(bf16)
    d_av = (da * sig_a * mask).astype(bf16)
    quarter = total // 4
    sums = (
        jnp.dot(zn_t, d_ag, preferred_element_type=f32),
        jnp.dot(zn_t, d_av, preferred_element_type=f32),
        b_sums[0],
        b_sums[1],
    )
    for at, term in enumerate(sums):
        w_part[at * quarter : (at + 1) * quarter, share : 3 * share] = (
            term.astype(bf16).reshape(quarter, 2 * share, width))
    scatter_weights(0, w_part, w_recv)
    dzn = dot_t(dg, w_gate_ref[...]) + dot_t(d_ag, w_in_ref[:, 0:width])
    dzn = dzn + dot_t(d_av, w_in_ref[:, width : 2 * width])
    w_stage(0, w_recv).wait_recv()
    w_all[me] = jnp.sum(w_recv[...].astype(f32), axis=0).astype(bf16)
    for step in peers:
        _, target = peer(step)
        w_copy(1, w_all.at[me], w_all.at[me], target).start()

    db = db_send[row].astype(f32)
    for other in near[1:]:
        db_copy(other, other).wait_recv()
        db = db + db_recv[other].astype(f32)
    db = db.reshape(size, width)
    d_bg = (db * slope_g[row]).astype(bf16)
    d_bv = (db * slope_v[row]).astype(bf16)
    dzn = dzn + dot_t(d_bg, w_in_ref[:, 2 * width : 3 * width])
    dzn = dzn + dot_t(d_bv, w_in_ref[:, 3 * width : 4 * width])
    zhat, zinv = normed(row)
    scaled = dzn * gain_in_ref[...]
    pair_grad = zinv * (scaled - last_mean(scaled) - zhat * last_mean(scaled * zhat))
    pair_grad_ref[...] = pair_grad.astype(bf16).reshape(blk, blk, width)

    for step in range(1, n):
        pair_copy(row, lax.rem(row + step, n)).wait_send()
        dx_copy(col, lax.rem(col + step, n)).wait_send()
        x_copy(lax.rem(col + step, n), col).wait_send()
        db_copy(lax.rem(row + step, n), row).wait_send()
    w_stage(0, w_part).wait_send()
    w_stage(1, w_all).wait_recv()
    early = w_all[:, 0:share].reshape(2 * width, width).astype(f32)
    grad_gate_ref[...], grad_out_ref[...] = early[:width], early[width:]
    late = w_all[:, share : 3 * share].reshape(4 * width, width).astype(f32)
    for at in range(4):
        grad_in_ref[:, at * width : (at + 1) * width] = late[at * width : (at + 1) * width]
    w_stage(1, w_all).wait_send()


def store_kernel(*refs):
    sources, targets, sems = refs[:5], refs[5:10], refs[10]
    copies = [
        pltpu.make_async_copy(source, target, sems.at[at])
        for at, (source, target) in enumerate(zip(sources, targets))
    ]
    for copy in copies:
        copy.start()
    for copy in copies:
        copy.wait()


def fused_plan(n, pair, cotangent, crop_length, gain_in, w_in, w_gate, product_norm_gain, w_out):
    blk, _, width = pair.shape
    total = n * n
    share = 2 * width // total
    f32, bf16 = jnp.float32, jnp.bfloat16
    shape = jax.ShapeDtypeStruct
    blocks = (n, blk, blk, width)
    grad = lambda rows: pltpu.VMEM((total, rows, width), bf16)
    slope = pltpu.VMEM((n, blk * blk, width), f32)
    dma = pltpu.SemaphoreType.DMA
    vmem = pl.BlockSpec(memory_space=pltpu.VMEM)
    hbm = pl.BlockSpec(memory_space=pltpu.HBM)
    out_shape = (
        shape(pair.shape, bf16),
        shape(pair.shape, bf16),
        shape(w_in.shape, f32),
        shape(w_gate.shape, f32),
        shape(w_out.shape, f32),
    )
    results = pl.pallas_call(
        functools.partial(fused_kernel, n),
        out_shape=out_shape,
        in_specs=[pl.BlockSpec(memory_space=pltpu.SMEM)] + [hbm] * 7,
        out_specs=(vmem,) * 5,
        scratch_shapes=[
            pltpu.VMEM(blocks, bf16),
            pltpu.VMEM(blocks, bf16),
            pltpu.VMEM(blocks, bf16),
            pltpu.VMEM(blocks, bf16),
            pltpu.VMEM(blocks, bf16),
            pltpu.VMEM(blocks, bf16),
            pltpu.VMEM(blocks, bf16),
            grad(3 * share),
            grad(3 * share),
            grad(3 * share),
            pltpu.VMEM((n, width, blk * blk), bf16),
            slope,
            slope,
            pltpu.VMEM((2, width, width), f32),
            pltpu.VMEM(pair.shape, bf16),
            pltpu.VMEM((1, width), f32),
            pltpu.VMEM(w_in.shape, bf16),
            pltpu.VMEM(w_gate.shape, bf16),
            pltpu.VMEM((1, width), f32),
            pltpu.VMEM(w_out.shape, bf16),
            pltpu.VMEM(blocks[1:], f32),
            pltpu.VMEM(blocks[1:], f32),
            pltpu.VMEM(blocks[1:], f32),
            pltpu.VMEM(blocks[1:], f32),
            pltpu.VMEM((blk * blk, 2 * width), f32),
        ]
        + [dma((n,))] * 8
        + [dma((2,))] * 2
        + [dma((7,))],
        compiler_params=pltpu.CompilerParams(
            collective_id=0, has_side_effects=True, vmem_limit_bytes=VMEM_GRANT
        ),
    )(
        crop_length,
        pair,
        cotangent,
        gain_in.reshape(1, width),
        w_in,
        w_gate,
        product_norm_gain.reshape(1, width),
        w_out,
    )
    return pl.pallas_call(
        store_kernel,
        out_shape=out_shape,
        in_specs=[vmem] * 5,
        out_specs=(hbm,) * 5,
        scratch_shapes=[dma((5,))],
    )(*results)


def choose_plan(n_rows, n_cols, pair, cotangent, crop_length, gain_in, w_in, w_gate, product_norm_gain, w_out):
    args = (pair, cotangent, crop_length, gain_in, w_in, w_gate, product_norm_gain, w_out)
    square = n_rows == n_cols and pair.shape[0] == pair.shape[1] == 16
    even = w_in.shape == (128, 512) and 256 % (16 * n_rows * n_cols) == 0
    return fused_plan(n_rows, *args) if square and even else per_device(*args)


def solution(mesh):
    in_specs = (
        P(("groups", "rows"), "cols", None),
        P(("groups", "rows"), "cols", None),
        P("groups"),
        P(),
        P(),
        P(),
        P(),
        P(),
    )
    out_specs = (
        P(("groups", "rows"), "cols", None),
        P(("groups", "rows"), "cols", None),
        P("groups", None),
        P("groups", None),
        P("groups", None),
    )
    return jax.shard_map(
        functools.partial(choose_plan, mesh.shape["rows"], mesh.shape["cols"]), mesh=mesh, in_specs=in_specs, out_specs=out_specs, check_vma=False
    )
```

```python
import functools

import jax
import jax.numpy as jnp
from jax import lax
from jax.experimental import pallas as pl
from jax.experimental.pallas import tpu as pltpu
from jax.sharding import PartitionSpec as P


def apply_layer_norm(values, gain):
    centre = values - jnp.mean(values, axis=-1, keepdims=True)
    inverse = lax.rsqrt(jnp.mean(centre * centre, axis=-1, keepdims=True) + 1e-05)
    normed = centre * inverse
    return (normed * gain, normed, inverse)


def layer_norm_backward(upstream, gain, normed, inverse):
    scaled = upstream * gain
    return inverse * (
        scaled
        - jnp.mean(scaled, axis=-1, keepdims=True)
        - normed * jnp.mean(scaled * normed, axis=-1, keepdims=True)
    )


def per_device(pair, cotangent, crop_length, gain_in, w_in, w_gate, product_norm_gain, w_out):
    f32 = jnp.float32
    to_brain_float = jnp.bfloat16
    row_count = pair.shape[0]
    col_count = pair.shape[1]
    hidden_width = w_out.shape[0]
    row_ids = lax.axis_index("rows") * row_count + jnp.arange(row_count, dtype=jnp.int32)
    col_ids = lax.axis_index("cols") * col_count + jnp.arange(col_count, dtype=jnp.int32)
    row_valid = (row_ids < crop_length[0]).astype(f32)
    col_valid = (col_ids < crop_length[0]).astype(f32)
    mask = (row_valid[:, None] * col_valid[None, :])[:, :, None]
    zn_full, zhat, zinv = apply_layer_norm(pair.astype(f32), gain_in)
    zn_b = zn_full.astype(to_brain_float)
    proj = jnp.dot(zn_b, w_in, preferred_element_type=f32)
    gate = jnp.dot(zn_b, w_gate, preferred_element_type=f32)
    pa_g = proj[..., 0:hidden_width]
    pa_v = proj[..., hidden_width : 2 * hidden_width]
    pb_g = proj[..., 2 * hidden_width : 3 * hidden_width]
    pb_v = proj[..., 3 * hidden_width : 4 * hidden_width]
    sig_a = jax.nn.sigmoid(pa_g)
    sig_b = jax.nn.sigmoid(pb_g)
    left = (sig_a * pa_v * mask).astype(to_brain_float)
    right = (sig_b * pb_v * mask).astype(to_brain_float)
    right_all = lax.all_gather(right, "rows", axis=0, tiled=True)
    partial_value = jnp.einsum("ikh,jkh->ijh", left, right_all, preferred_element_type=f32)
    triangle_update = lax.psum_scatter(
        partial_value.astype(jnp.bfloat16), "cols", scatter_dimension=1, tiled=True
    ).astype(jnp.float32)
    normed_input_full, centred_input, inverse_deviation = apply_layer_norm(
        triangle_update, product_norm_gain
    )
    xn_b = normed_input_full.astype(to_brain_float)
    q_out = jnp.dot(xn_b, w_out, preferred_element_type=f32)
    sig_g = jax.nn.sigmoid(gate)
    update = (sig_g * q_out).astype(to_brain_float)
    upstream = cotangent.astype(f32)
    dq_b = (upstream * sig_g).astype(to_brain_float)
    dg_b = (upstream * q_out * sig_g * (1.0 - sig_g)).astype(to_brain_float)
    local_out = jnp.einsum("ijc,ijd->cd", xn_b, dq_b, preferred_element_type=f32)
    normed_input_grad = jnp.dot(dq_b, w_out.T, preferred_element_type=f32)
    input_grad_piece = layer_norm_backward(
        normed_input_grad, product_norm_gain, centred_input, inverse_deviation
    ).astype(to_brain_float)
    dx_row = lax.all_gather(input_grad_piece, "cols", axis=1, tiled=True)
    grad_left = jnp.einsum("ijh,jkh->ikh", dx_row, right_all, preferred_element_type=f32)
    right_terms = jnp.einsum("ijh,ikh->jkh", dx_row, left, preferred_element_type=f32)
    grad_right = lax.psum_scatter(
        right_terms.astype(jnp.bfloat16), "rows", scatter_dimension=0, tiled=True
    ).astype(jnp.float32)
    dproj = jnp.concatenate(
        [
            grad_left * pa_v * mask * sig_a * (1.0 - sig_a),
            grad_left * sig_a * mask,
            grad_right * pb_v * mask * sig_b * (1.0 - sig_b),
            grad_right * sig_b * mask,
        ],
        axis=-1,
    ).astype(to_brain_float)
    local_in = jnp.einsum("ijc,ijd->cd", zn_b, dproj, preferred_element_type=f32)
    local_gate = jnp.einsum("ijc,ijd->cd", zn_b, dg_b, preferred_element_type=f32)
    grad_in, grad_gate, grad_out = lax.psum((local_in, local_gate, local_out), ("rows", "cols"))
    dzn = jnp.dot(dproj, w_in.T, preferred_element_type=f32) + jnp.dot(
        dg_b, w_gate.T, preferred_element_type=f32
    )
    pair_grad = layer_norm_backward(dzn, gain_in, zhat, zinv).astype(to_brain_float)
    return (update, pair_grad, grad_in, grad_gate, grad_out)


VMEM_GRANT = 63 * 1024 * 1024
MESH = pl.DeviceIdType.MESH


def last_mean(values):
    return jnp.mean(values, axis=-1, keepdims=True)


def dot_t(lhs, rhs):
    return lax.dot_general(lhs, rhs, (((1,), (1,)), ((), ())), preferred_element_type=jnp.float32)


def fused_kernel(
    n,
    crop_ref,
    pair_hbm,
    cot_hbm,
    gain_in_hbm,
    w_in_hbm,
    w_gate_hbm,
    gain_x_hbm,
    w_out_hbm,
    update_ref,
    pair_grad_ref,
    grad_in_ref,
    grad_gate_ref,
    grad_out_ref,
    pair_all,
    b_all,
    x_send,
    x_recv,
    dx_all,
    db_send,
    db_recv,
    w_part,
    w_recv,
    w_all,
    zn_all,
    slope_g,
    slope_v,
    b_sums,
    cot_ref,
    gain_in_ref,
    w_in_ref,
    w_gate_ref,
    gain_x_ref,
    w_out_ref,
    left_f,
    right_f,
    dx_f,
    da_f,
    proj_ref,
    pair_ss,
    pair_rs,
    x_ss,
    x_rs,
    dx_ss,
    dx_rs,
    db_ss,
    db_rs,
    w_ss,
    w_rs,
    in_sem,
):
    f32, bf16 = jnp.float32, jnp.bfloat16
    blk, _, width = pair_hbm.shape
    size = blk * blk
    total = n * n
    share = 2 * width // total
    row = lax.axis_index("rows")
    col = lax.axis_index("cols")
    me = row * n + col

    def peer(steps):
        to_row, to_col = lax.rem(row + steps[0], n), lax.rem(col + steps[1], n)
        return to_row * n + to_col, {"rows": to_row, "cols": to_col}

    far_first = sorted(range(1, n), key=lambda step: -min(step, n - step))
    peers = [(r, c) for c in far_first + [0] for r in range(n) if r + c > 0]

    def nearest(place):
        for step in range(0, n, 2):
            base = lax.rem(place + step, n)
            yield base
            yield base + 1 - 2 * lax.rem(base, 2)

    near = list(nearest(row))

    fetches = [
        pltpu.make_async_copy(source, target, in_sem.at[at])
        for at, (source, target) in enumerate([
            (pair_hbm, pair_all.at[row]),
            (gain_in_hbm, gain_in_ref),
            (w_in_hbm, w_in_ref),
            (w_gate_hbm, w_gate_ref),
            (cot_hbm, cot_ref),
            (w_out_hbm, w_out_ref),
            (gain_x_hbm, gain_x_ref),
        ])
    ]
    for fetch in fetches:
        fetch.start()

    barrier = pltpu.get_barrier_semaphore()
    for step in peers:
        _, target = peer(step)
        pl.semaphore_signal(barrier, inc=1, device_id=target, device_id_type=MESH)

    def pair_copy(slot, other):
        return pltpu.make_async_remote_copy(
            pair_all.at[slot], pair_all.at[slot], pair_ss.at[other], pair_rs.at[slot],
            device_id={"rows": other}, device_id_type=MESH)

    def x_copy(block, slot):
        return pltpu.make_async_remote_copy(
            x_send.at[block], x_recv.at[slot], x_ss.at[block], x_rs.at[slot],
            device_id={"cols": block}, device_id_type=MESH)

    def dx_copy(slot, other):
        return pltpu.make_async_remote_copy(
            dx_all.at[slot], dx_all.at[slot], dx_ss.at[other], dx_rs.at[slot],
            device_id={"cols": other}, device_id_type=MESH)

    def db_copy(block, slot):
        return pltpu.make_async_remote_copy(
            db_send.at[block], db_recv.at[slot], db_ss.at[block], db_rs.at[slot],
            device_id={"rows": block}, device_id_type=MESH)

    def w_copy(stage, source, target, device):
        return pltpu.make_async_remote_copy(
            source, target, w_ss.at[stage], w_rs.at[stage],
            device_id=device, device_id_type=MESH)

    def w_stage(stage, buffer):
        piece = buffer.at[pl.ds(0, total - 1)]
        return w_copy(stage, piece, piece, peer(peers[0])[1])

    def scatter_weights(stage, outgoing, arriving):
        for step in peers:
            other, target = peer(step)
            w_copy(stage, outgoing.at[other], arriving.at[me], target).start()
        arriving[me] = outgoing[me]

    crop = crop_ref[0]
    place = lax.broadcasted_iota(jnp.int32, (size, width), 0)
    row_ids = lax.div(place, blk)
    col_ok = col * blk + lax.rem(place, blk) < crop

    def mask_of(block):
        return jnp.where((block * blk + row_ids < crop) & col_ok, 1.0, 0.0).astype(f32)

    def normed(block):
        pair = pair_all[block].reshape(size, width).astype(f32)
        centre = pair - last_mean(pair)
        zinv = lax.rsqrt(last_mean(centre * centre) + 1e-05)
        return centre * zinv, zinv

    def prepare(block):
        zhat, _ = normed(block)
        zn_f = zhat * gain_in_ref[...]
        zn = zn_f.astype(bf16)
        mask = mask_of(block)
        pb = jnp.dot(zn, w_in_ref[:, 2 * width : 4 * width], preferred_element_type=f32)
        gated = jax.nn.sigmoid(pb[:, :width]) * mask
        right = (gated * pb[:, width:]).astype(bf16)
        b_all[block] = right.reshape(blk, blk, width)
        slope_g[block] = pb[:, :width]
        slope_v[block] = pb[:, width:]
        return zn

    def prepare_backward(block):
        zn_all[block] = (normed(block)[0] * gain_in_ref[...]).T.astype(bf16)
        sig = jax.nn.sigmoid(slope_g[block])
        gated = sig * mask_of(block)
        slope_g[block] = gated * slope_v[block] * (1.0 - sig)
        slope_v[block] = gated

    for fetch in fetches[:4]:
        fetch.wait()
    zn = prepare(row)
    pl.semaphore_wait(barrier, total - 1)
    for other in near[1:]:
        pair_copy(row, other).start()

    mask = mask_of(row)
    proj_ref[...] = jnp.dot(zn, w_in_ref[:, 0 : 2 * width], preferred_element_type=f32)
    sig_a = jax.nn.sigmoid(proj_ref[:, 0:width])
    left = (sig_a * proj_ref[:, width : 2 * width] * mask).astype(bf16).astype(f32)
    left_f[...] = left.reshape(blk, blk, width)
    sig_g = jax.nn.sigmoid(jnp.dot(zn, w_gate_ref[...], preferred_element_type=f32))

    for step, block in enumerate(near):
        if step > 0:
            pair_copy(block, block).wait_recv()
            prepare(block)
        right_f[...] = jnp.swapaxes(b_all[block].astype(f32), 0, 1)

        @pl.loop(0, blk, unroll=4)
        def _(i):
            line = left_f[i]
            x_send[block, i] = jnp.sum(line[:, None, :] * right_f[...], axis=0).astype(bf16)

        @pl.when(block != col)
        def _():
            x_copy(block, col).start()

    for block in near:
        prepare_backward(block)
    x = x_send[col].astype(f32)
    for step in range(1, n):
        other = lax.rem(col + step, n)
        x_copy(other, other).wait_recv()
        x = x + x_recv[other].astype(f32)
    x = x.reshape(size, width)

    for fetch in fetches[4:]:
        fetch.wait()
    gain_x = gain_x_ref[...]
    w_out = w_out_ref[...]
    cot = cot_ref[...].reshape(size, width).astype(f32)
    centre = x - last_mean(x)
    xinv = lax.rsqrt(last_mean(centre * centre) + 1e-05)
    xhat = centre * xinv
    xn_f = xhat * gain_x
    dq = (cot * sig_g).astype(bf16)
    scaled = dot_t(dq, w_out) * gain_x
    dx = xinv * (scaled - last_mean(scaled) - xhat * last_mean(scaled * xhat))
    dx_all[col] = dx.astype(bf16).reshape(blk, blk, width)
    for step in far_first:
        dx_copy(col, lax.rem(col + step, n)).start()
    q_out = jnp.dot(xn_f.astype(bf16), w_out, preferred_element_type=f32)
    update_ref[...] = (sig_g * q_out).astype(bf16).reshape(blk, blk, width)
    dg = (cot * q_out * sig_g * (1.0 - sig_g)).astype(bf16)
    zn_t = zn_all[row]
    half = total // 2
    w_part[0:half, 0:share] = (
        jnp.dot(zn_t, dg, preferred_element_type=f32).astype(bf16).reshape(half, share, width))
    w_part[half:total, 0:share] = (
        jnp.dot(xn_f.T.astype(bf16), dq, preferred_element_type=f32)
        .astype(bf16).reshape(half, share, width))

    da_f[...] = jnp.zeros_like(da_f)
    b_sums[...] = jnp.zeros_like(b_sums)
    for step in [0] + far_first[::-1]:
        block = lax.rem(col + step, n)
        if step > 0:
            dx_copy(block, block).wait_recv()
        dx_f[...] = dx_all[block].astype(f32)
        right_f[...] = b_all[block].astype(f32)

        def over_i(i, db):
            line = dx_f[i][:, None, :]
            da_f[i] += jnp.sum(line * right_f[...], axis=0)
            return db + line * left_f[i][None]

        db = lax.fori_loop(0, blk, over_i, jnp.zeros((blk, blk, width), f32), unroll=2)
        db_send[block] = db.astype(bf16)

        @pl.when(block != row)
        def _():
            db_copy(block, row).start()

        terms = db.reshape(size, width)
        zn_block = zn_all[block]
        b_sums[0] += jnp.dot(
            zn_block, (terms * slope_g[block]).astype(bf16), preferred_element_type=f32)
        b_sums[1] += jnp.dot(
            zn_block, (terms * slope_v[block]).astype(bf16), preferred_element_type=f32)

    da = da_f[...].reshape(size, width)
    pa_v = proj_ref[:, width : 2 * width]
    d_ag = (da * pa_v * mask * sig_a * (1.0 - sig_a)).astype(bf16)
    d_av = (da * sig_a * mask).astype(bf16)
    quarter = total // 4
    sums = (
        jnp.dot(zn_t, d_ag, preferred_element_type=f32),
        jnp.dot(zn_t, d_av, preferred_element_type=f32),
        b_sums[0],
        b_sums[1],
    )
    for at, term in enumerate(sums):
        w_part[at * quarter : (at + 1) * quarter, share : 3 * share] = (
            term.astype(bf16).reshape(quarter, 2 * share, width))
    scatter_weights(0, w_part, w_recv)
    dzn = dot_t(dg, w_gate_ref[...]) + dot_t(d_ag, w_in_ref[:, 0:width])
    dzn = dzn + dot_t(d_av, w_in_ref[:, width : 2 * width])
    w_stage(0, w_recv).wait_recv()
    w_all[me] = jnp.sum(w_recv[...].astype(f32), axis=0).astype(bf16)
    for step in peers:
        _, target = peer(step)
        w_copy(1, w_all.at[me], w_all.at[me], target).start()

    db = db_send[row].astype(f32)
    for other in near[1:]:
        db_copy(other, other).wait_recv()
        db = db + db_recv[other].astype(f32)
    db = db.reshape(size, width)
    d_bg = (db * slope_g[row]).astype(bf16)
    d_bv = (db * slope_v[row]).astype(bf16)
    dzn = dzn + dot_t(d_bg, w_in_ref[:, 2 * width : 3 * width])
    dzn = dzn + dot_t(d_bv, w_in_ref[:, 3 * width : 4 * width])
    zhat, zinv = normed(row)
    scaled = dzn * gain_in_ref[...]
    pair_grad = zinv * (scaled - last_mean(scaled) - zhat * last_mean(scaled * zhat))
    pair_grad_ref[...] = pair_grad.astype(bf16).reshape(blk, blk, width)

    for step in range(1, n):
        pair_copy(row, lax.rem(row + step, n)).wait_send()
        dx_copy(col, lax.rem(col + step, n)).wait_send()
        x_copy(lax.rem(col + step, n), col).wait_send()
        db_copy(lax.rem(row + step, n), row).wait_send()
    w_stage(0, w_part).wait_send()
    w_stage(1, w_all).wait_recv()
    early = w_all[:, 0:share].reshape(2 * width, width).astype(f32)
    grad_gate_ref[...], grad_out_ref[...] = early[:width], early[width:]
    late = w_all[:, share : 3 * share].reshape(4 * width, width).astype(f32)
    for at in range(4):
        grad_in_ref[:, at * width : (at + 1) * width] = late[at * width : (at + 1) * width]
    w_stage(1, w_all).wait_send()


def store_kernel(*refs):
    sources, targets, sems = refs[:5], refs[5:10], refs[10]
    copies = [
        pltpu.make_async_copy(source, target, sems.at[at])
        for at, (source, target) in enumerate(zip(sources, targets))
    ]
    for copy in copies:
        copy.start()
    for copy in copies:
        copy.wait()


def fused_plan(n, pair, cotangent, crop_length, gain_in, w_in, w_gate, product_norm_gain, w_out):
    blk, _, width = pair.shape
    total = n * n
    share = 2 * width // total
    f32, bf16 = jnp.float32, jnp.bfloat16
    shape = jax.ShapeDtypeStruct
    blocks = (n, blk, blk, width)
    grad = lambda rows: pltpu.VMEM((total, rows, width), bf16)
    slope = pltpu.VMEM((n, blk * blk, width), f32)
    dma = pltpu.SemaphoreType.DMA
    vmem = pl.BlockSpec(memory_space=pltpu.VMEM)
    hbm = pl.BlockSpec(memory_space=pltpu.HBM)
    out_shape = (
        shape(pair.shape, bf16),
        shape(pair.shape, bf16),
        shape(w_in.shape, f32),
        shape(w_gate.shape, f32),
        shape(w_out.shape, f32),
    )
    results = pl.pallas_call(
        functools.partial(fused_kernel, n),
        out_shape=out_shape,
        in_specs=[pl.BlockSpec(memory_space=pltpu.SMEM)] + [hbm] * 7,
        out_specs=(vmem,) * 5,
        scratch_shapes=[
            pltpu.VMEM(blocks, bf16),
            pltpu.VMEM(blocks, bf16),
            pltpu.VMEM(blocks, bf16),
            pltpu.VMEM(blocks, bf16),
            pltpu.VMEM(blocks, bf16),
            pltpu.VMEM(blocks, bf16),
            pltpu.VMEM(blocks, bf16),
            grad(3 * share),
            grad(3 * share),
            grad(3 * share),
            pltpu.VMEM((n, width, blk * blk), bf16),
            slope,
            slope,
            pltpu.VMEM((2, width, width), f32),
            pltpu.VMEM(pair.shape, bf16),
            pltpu.VMEM((1, width), f32),
            pltpu.VMEM(w_in.shape, bf16),
            pltpu.VMEM(w_gate.shape, bf16),
            pltpu.VMEM((1, width), f32),
            pltpu.VMEM(w_out.shape, bf16),
            pltpu.VMEM(blocks[1:], f32),
            pltpu.VMEM(blocks[1:], f32),
            pltpu.VMEM(blocks[1:], f32),
            pltpu.VMEM(blocks[1:], f32),
            pltpu.VMEM((blk * blk, 2 * width), f32),
        ]
        + [dma((n,))] * 8
        + [dma((2,))] * 2
        + [dma((7,))],
        compiler_params=pltpu.CompilerParams(
            collective_id=0, has_side_effects=True, vmem_limit_bytes=VMEM_GRANT
        ),
    )(
        crop_length,
        pair,
        cotangent,
        gain_in.reshape(1, width),
        w_in,
        w_gate,
        product_norm_gain.reshape(1, width),
        w_out,
    )
    return pl.pallas_call(
        store_kernel,
        out_shape=out_shape,
        in_specs=[vmem] * 5,
        out_specs=(hbm,) * 5,
        scratch_shapes=[dma((5,))],
    )(*results)


def choose_plan(n_rows, n_cols, pair, cotangent, crop_length, gain_in, w_in, w_gate, product_norm_gain, w_out):
    args = (pair, cotangent, crop_length, gain_in, w_in, w_gate, product_norm_gain, w_out)
    square = n_rows == n_cols and pair.shape[0] == pair.shape[1] == 16
    even = w_in.shape == (128, 512) and 256 % (16 * n_rows * n_cols) == 0
    return fused_plan(n_rows, *args) if square and even else per_device(*args)


def solution(mesh):
    in_specs = (
        P(("groups", "rows"), "cols", None),
        P(("groups", "rows"), "cols", None),
        P("groups"),
        P(),
        P(),
        P(),
        P(),
        P(),
    )
    out_specs = (
        P(("groups", "rows"), "cols", None),
        P(("groups", "rows"), "cols", None),
        P("groups", None),
        P("groups", None),
        P("groups", None),
    )
    return jax.shard_map(
        functools.partial(choose_plan, mesh.shape["rows"], mesh.shape["cols"]), mesh=mesh, in_specs=in_specs, out_specs=out_specs, check_vma=False
    )
```
